32 devices in a mesh: dp: 2 (over x), expert: 4 (over y, core), mp: 4 (over z).
Axes of the slice: x: 2, y: 2, z: 4, core: 2. Of those that a mesh axis runs over, the one named last changes fastest.
Arguments:
- tokens: bfloat16 [128, 3072], P('dp'), may hold values from -6 to 6
- expert_ids: int32 [128, 2], P('dp'), may hold values from 0 to 3, all different within a row; in each aligned block of 64 rows (0 to 63, 64 to 127, ...) at most 64 rows name the same one
- gate_values: float32 [128, 2], P('dp'), may hold values from 0.2 to 1
- targets: int32 [128], P('dp'), may hold values from 0 to 32767
- w_gate: bfloat16 [4, 3072, 4, 2048], P('expert', None, 'mp', 'dp'), may hold values from -0.109375 to 0.109375
- w_up: bfloat16 [4, 3072, 4, 2048], P('expert', None, 'mp', 'dp'), may hold values from -0.109375 to 0.109375
- w_down: bfloat16 [4, 4, 2048, 3072], P('expert', 'mp', None, 'dp'), may hold values from -0.0625 to 0.0625
- norm_gain: float32 [3072], replicated, may hold values from 0.1 to 1.9
- lens_head: bfloat16 [3072, 32768], P('dp', ('expert', 'mp')), may hold values from -120 to 120
Outputs:
- mixed: bfloat16 [128, 3072], P('dp')
- log_probs: float32 [128], P('dp')
The draws below stay inside these ranges and needn't reach their ends.
Inputs may be any that keep to these rules, and one draw needn't show every extreme that they name: `expert_ids`: each row names two different experts; in each aligned block of 64 rows no expert is named by more than 64 rows, a bound that some block reaches.
All inputs are finite; a program needn't handle non-finite values.
Results may differ from the reference program's by a relative error of at most 0.0041.
Values may be sent and summed in bfloat16 or wider, within the bound.
A program may use at most 128 MiB of HBM per device.

```python
import math
import jax
import jax.numpy as jnp
import numpy as np
from jax import lax

D = 3072
FF = 8192
VOCAB = 32768
EXPERTS = 4
TOK_DP = 64
CAP = 64
TOKENS = 128
N_DP = 2
N_MP = 4


def draw_lens_head(key, part):
    key_base, key_scale = jax.random.split(key, 2)
    normal_part = jnp.clip(jax.random.normal(key_base, (D, VOCAB), jnp.float32), -6.0, 6.0)
    columns = jnp.arange(VOCAB, dtype=jnp.float32)
    col_scale = jnp.exp(jax.random.uniform(key_scale, (VOCAB,), jnp.float32, math.log(0.7), math.log(1.4)))
    col_scale = col_scale * (1.0 + 0.6 * columns / VOCAB)
    base = normal_part * col_scale[None, :] / math.sqrt(D)
    return base.astype(jnp.bfloat16)


def with_ends(drawn, rng, least, largest):
    longest = drawn.shape.index(max(drawn.shape))
    spots = []
    for shift in (0, 1):
        where = [jax.random.randint(jax.random.fold_in(rng, axis), (), 0, length) for axis, length in enumerate(drawn.shape)]
        where[longest] = (where[longest] + shift) % drawn.shape[longest]
        spots.append(tuple(where))
    return drawn.at[spots[0]].set(least).at[spots[1]].set(largest)


def level_of(key, dims, shards, low, largest):
    def one(position, blocks):
        draws = jax.random.uniform(jax.random.fold_in(jax.random.fold_in(key, 6), position), (blocks,), jnp.float32, low / len(shards), largest / len(shards))
        return jnp.repeat(jnp.exp(draws), dims[position] // blocks).reshape((-1,) + (1,) * (len(dims) - position - 1))

    loudness = one(*shards[0])
    for cut in shards[1:]:
        loudness = loudness * one(*cut)
    return loudness


def routed_block(rng, own, number, rows, count, top, most, slope):
    ranking = jax.random.permutation(rng, count)
    crowded, ordinary = load_shares(count, rows * top, most, slope, True), load_shares(count, rows * top, most, slope, False)
    places = jnp.arange(count)

    def named(lengths, rotation):
        used = int((lengths > 0).sum())
        fixed = max(1, used // 4)
        shifted = fixed + (places - fixed + rotation * (used - fixed)) % max(1, count - fixed)
        return jnp.zeros((count,), jnp.int32).at[ranking[jnp.where(places < fixed, places, shifted)]].set(jnp.asarray(lengths, jnp.int32))

    lengths = jnp.where(number % 4 == 0, named(crowded, number // 4), named(ordinary, number - number // 4 - 1))
    mixed = jax.random.permutation(jax.random.fold_in(own, 3), count)
    giver, sink = mixed[0:count // 2 * 2:2], mixed[1:count // 2 * 2:2]
    margin = jnp.minimum(lengths[giver] - 1, most - lengths[sink]) // 2
    margin = jnp.where((giver == ranking[0]) | (sink == ranking[0]) | (lengths[sink] == 0), 0, jnp.maximum(margin, 0))
    shifted = jax.random.randint(jax.random.fold_in(own, 4), (count // 2,), 0, 1 << 20) % (margin + 1)
    lengths = lengths.at[giver].add(-shifted).at[sink].add(shifted)
    labels = jnp.searchsorted(jnp.cumsum(lengths), jnp.arange(rows * top), side="right").astype(jnp.int32)
    table = labels.reshape(top, rows).T
    table = table[jax.random.permutation(jax.random.fold_in(own, 1), rows)]
    rotation = jax.random.randint(jax.random.fold_in(own, 2), (rows, 1), 0, top)
    return jnp.take_along_axis(table, (jnp.arange(top)[None, :] + rotation) % top, axis=1)


def load_shares(count, total, most, slope, full):
    portions = [(1 << 20) // math.isqrt(standing ** slope) + 1 for standing in range(1, count + 1)]
    largest = most if full else min(most, max(-(-total // count), total * portions[0] // sum(portions)))
    least = 1 if total - largest >= count - 1 else 0
    counts, spare = [largest] + [least] * (count - 1), total - largest - least * (count - 1)
    while spare > 0:
        candidates = [i for i in range(1, count) if counts[i] < largest] or [i for i in range(1, count) if counts[i] < most]
        pool, remaining = sum([portions[i] for i in candidates]), spare
        for i in candidates:
            addition = min(most - counts[i], max(1, remaining * portions[i] // pool), spare)
            counts[i] = counts[i] + addition
            spare = spare - addition
    return np.array(counts)


def centred(key, shape, deviation, reach, cuts=(), kind=jnp.bfloat16):
    loudness = level_of(key, shape, cuts, -0.22, 0.18) if cuts else 1.0
    drawn = jax.random.normal(key, shape, jnp.float32) * deviation * loudness
    return jnp.minimum(jnp.maximum(drawn, -reach), reach).astype(kind)


def setup_inputs(seed: int = 0) -> dict:
    seeds = jax.random.split(jax.random.key(seed), 10)
    tokens = centred(seeds[0], (TOKENS, D), 1.0, 6.0, ((0, 2),))
    expert_ids_keys = jax.random.split(jax.random.fold_in(seeds[1], 1), TOKENS // TOK_DP)
    expert_ids_turns = jax.random.permutation(jax.random.fold_in(seeds[1], 3), TOKENS // TOK_DP)
    expert_ids = jax.vmap(lambda own, number: routed_block(jax.random.fold_in(seeds[1], 2), own, number, TOK_DP, EXPERTS, 2, CAP, 2))(expert_ids_keys, expert_ids_turns).reshape((TOKENS, 2))
    gate_values = jnp.clip(0.2 + 0.8 * jax.random.uniform(seeds[2], (TOKENS, 2), jnp.float32) ** level_of(seeds[2], (TOKENS, 2), ((0, 2),), -0.2, 0.2), 0.2, 1.0)
    targets = with_ends(jax.random.randint(seeds[3], (TOKENS,), 0, VOCAB), jax.random.fold_in(seeds[3], 1), 0, VOCAB - 1).astype(jnp.int32)
    w_gate = centred(seeds[4], (EXPERTS, D, N_MP, FF // N_MP), D ** -0.5, 0.109375, ((0, 4), (2, 4), (3, 2)))
    w_up = centred(seeds[5], (EXPERTS, D, N_MP, FF // N_MP), D ** -0.5, 0.109375, ((0, 4), (2, 4), (3, 2)))
    w_down = centred(seeds[6], (EXPERTS, N_MP, FF // N_MP, D), FF ** -0.5, 0.0625, ((0, 4), (1, 4), (3, 2)))
    norm_gain = jnp.clip(1.0 + 0.18 * jax.random.normal(seeds[7], (D,), jnp.float32), 0.1, 1.9)
    lens_head = draw_lens_head(jax.random.fold_in(seeds[9], 71), 0)
    return {"tokens": tokens, "expert_ids": expert_ids, "gate_values": gate_values, "targets": targets, "w_gate": w_gate, "w_up": w_up, "w_down": w_down, "norm_gain": norm_gain, "lens_head": lens_head}


def reference(tokens, expert_ids, gate_values, targets, w_gate, w_up, w_down, norm_gain, lens_head):
    gate_all = w_gate.reshape(EXPERTS, D, FF)
    up_all = w_up.reshape(EXPERTS, D, FF)
    down_all = w_down.reshape(EXPERTS, FF, D)
    slot_total = N_DP * CAP

    def one_expert(running, expert):
        matches = expert_ids == expert
        chosen = jnp.any(matches, axis=1)
        weights = lax.optimization_barrier(jnp.sum(jnp.where(matches, gate_values, jnp.float32(0.0)), axis=1))
        row_index = jnp.nonzero(chosen, size=slot_total, fill_value=0)[0].astype(jnp.int32)
        in_use = jnp.arange(slot_total, dtype=jnp.int32) < jnp.sum(chosen.astype(jnp.int32))
        picked = tokens[row_index]
        gate_part = jnp.dot(picked, gate_all[expert], preferred_element_type=jnp.float32)
        up_part = jnp.dot(picked, up_all[expert], preferred_element_type=jnp.float32)
        hidden = (jax.nn.silu(gate_part) * up_part).astype(jnp.bfloat16)
        expert_out = jnp.dot(hidden, down_all[expert], preferred_element_type=jnp.float32).astype(jnp.bfloat16)
        scaled = jnp.where(in_use[:, None], weights[row_index][:, None] * expert_out.astype(jnp.float32), jnp.float32(0.0))
        return (running.at[row_index].add(scaled), None)
    start_sum = jnp.zeros((TOKENS, D), jnp.float32)
    summed, _ = lax.scan(one_expert, start_sum, jnp.arange(EXPERTS, dtype=jnp.int32))
    mixed = (tokens.astype(jnp.float32) + summed).astype(jnp.bfloat16)
    mixed_f = mixed.astype(jnp.float32)
    scale = lax.rsqrt(lax.optimization_barrier(jnp.mean(mixed_f * mixed_f, axis=1, keepdims=True)) + 1e-05)
    normed = (mixed_f * scale * norm_gain.astype(jnp.float32)[None, :]).astype(jnp.bfloat16)
    logits = jnp.dot(normed, lens_head, preferred_element_type=jnp.float32)
    row_top = lax.optimization_barrier(jnp.max(logits, axis=1))
    exp_total = lax.optimization_barrier(jnp.sum(jnp.exp(logits - row_top[:, None]), axis=1))
    target_logit = jnp.take_along_axis(logits, targets.astype(jnp.int32)[:, None], axis=1)[:, 0]
    log_probs = target_logit - row_top - jnp.log(exp_total)
    return (mixed, log_probs)
```

```python
import jax
import jax.numpy as jnp
from jax import lax
from jax.sharding import PartitionSpec as P

f32, bf16 = jnp.float32, jnp.bfloat16


def per_device(
    tokens, expert_ids, gate_values, targets, w_gate, w_up, w_down, norm_gain, lens_head
):
    rows, feats = tokens.shape
    owner = lax.axis_index("expert")
    weights = jnp.sum(jnp.where(expert_ids == owner, gate_values, f32(0.0)), axis=1)
    gate_mat = w_gate.reshape(feats, -1)
    up_mat = w_up.reshape(feats, -1)
    down_mat = w_down.reshape(w_down.shape[2], w_down.shape[3])
    own_feats = down_mat.shape[1]
    all_tokens = lax.all_gather(tokens, "dp", axis=0, tiled=True)
    all_weights = lax.all_gather(weights, "dp", axis=0, tiled=True)
    gate_part = jnp.dot(all_tokens, gate_mat, preferred_element_type=f32)
    up_part = jnp.dot(all_tokens, up_mat, preferred_element_type=f32)
    hidden = (jax.nn.silu(gate_part) * up_part).astype(bf16)
    hidden = lax.all_gather(hidden, "dp", axis=1, tiled=True)
    part = jnp.dot(hidden, down_mat, preferred_element_type=f32) * all_weights[:, None]
    summed = lax.psum(part, ("expert", "mp"))
    first = lax.axis_index("dp") * own_feats
    own_tokens = lax.dynamic_slice_in_dim(all_tokens, first, own_feats, axis=1)
    own_gain = lax.dynamic_slice_in_dim(norm_gain, first, own_feats, axis=0)
    mixed_part = (own_tokens.astype(f32) + summed).astype(bf16)
    mixed = lax.all_to_all(mixed_part, "dp", split_axis=0, concat_axis=1, tiled=True)
    mixed_f = mixed.astype(f32)
    scale = lax.rsqrt(jnp.mean(mixed_f * mixed_f, axis=1) + 1e-05)
    gained = (mixed_part.astype(f32) * own_gain[None, :]).astype(bf16)
    logits_part = jnp.dot(gained, lens_head, preferred_element_type=f32)
    logits = lax.psum_scatter(logits_part, "dp", scatter_dimension=0, tiled=True)
    logits = logits * scale[:, None]
    vocab_cols = lens_head.shape[1]
    vocab_start = (owner * lax.axis_size("mp") + lax.axis_index("mp")) * vocab_cols
    columns = vocab_start + lax.broadcasted_iota(jnp.int32, (1, vocab_cols), 1)
    hit = columns == targets[:, None]
    target_local = jnp.sum(jnp.where(hit, logits, f32(0.0)), axis=1)
    top = jnp.max(logits, axis=1)
    total = jnp.sum(jnp.exp(logits - top[:, None]), axis=1)
    stats = lax.all_gather(jnp.stack([top, total, target_local]), ("expert", "mp"))
    tops, totals, hits = stats[:, 0], stats[:, 1], stats[:, 2]
    top_all = jnp.max(tops, axis=0)
    exp_total = jnp.sum(totals * jnp.exp(tops - top_all[None, :]), axis=0)
    log_probs = jnp.sum(hits, axis=0) - top_all - jnp.log(exp_total)
    return (mixed, log_probs)


def solution(mesh):
    in_specs = (
        P("dp", None),
        P("dp", None),
        P("dp", None),
        P("dp"),
        P("expert", None, "mp", "dp"),
        P("expert", None, "mp", "dp"),
        P("expert", "mp", None, "dp"),
        P(),
        P("dp", ("expert", "mp")),
    )
    out_specs = (P("dp", None), P("dp"))
    return jax.shard_map(
        per_device, mesh=mesh, in_specs=in_specs, out_specs=out_specs, check_vma=False
    )
```

```python
import jax
import jax.numpy as jnp
from jax import lax
from jax.experimental import pallas as pl
from jax.experimental.pallas import tpu as pltpu
from jax.sharding import PartitionSpec as P

f32, bf16 = jnp.float32, jnp.bfloat16


def per_device(
    tokens, expert_ids, gate_values, targets, w_gate, w_up, w_down, norm_gain, lens_head
):
    rows, feats = tokens.shape
    owner = lax.axis_index("expert")
    weights = jnp.sum(jnp.where(expert_ids == owner, gate_values, f32(0.0)), axis=1)
    gate_mat = w_gate.reshape(feats, -1)
    up_mat = w_up.reshape(feats, -1)
    down_mat = w_down.reshape(w_down.shape[2], w_down.shape[3])
    own_feats = down_mat.shape[1]
    all_tokens = lax.all_gather(tokens, "dp", axis=0, tiled=True)
    all_weights = lax.all_gather(weights, "dp", axis=0, tiled=True)
    gate_part = jnp.dot(all_tokens, gate_mat, preferred_element_type=f32)
    up_part = jnp.dot(all_tokens, up_mat, preferred_element_type=f32)
    hidden = (jax.nn.silu(gate_part) * up_part).astype(bf16)
    hidden = lax.all_gather(hidden, "dp", axis=1, tiled=True)
    part = jnp.dot(hidden, down_mat, preferred_element_type=f32) * all_weights[:, None]
    summed = lax.psum(part, ("expert", "mp"))
    first = lax.axis_index("dp") * own_feats
    own_tokens = lax.dynamic_slice_in_dim(all_tokens, first, own_feats, axis=1)
    own_gain = lax.dynamic_slice_in_dim(norm_gain, first, own_feats, axis=0)
    mixed_part = (own_tokens.astype(f32) + summed).astype(bf16)
    mixed = lax.all_to_all(mixed_part, "dp", split_axis=0, concat_axis=1, tiled=True)
    mixed_f = mixed.astype(f32)
    scale = lax.rsqrt(jnp.mean(mixed_f * mixed_f, axis=1) + 1e-05)
    gained = (mixed_part.astype(f32) * own_gain[None, :]).astype(bf16)
    logits_part = jnp.dot(gained, lens_head, preferred_element_type=f32)
    logits = lax.psum_scatter(logits_part, "dp", scatter_dimension=0, tiled=True)
    logits = logits * scale[:, None]
    vocab_cols = lens_head.shape[1]
    vocab_start = (owner * lax.axis_size("mp") + lax.axis_index("mp")) * vocab_cols
    columns = vocab_start + lax.broadcasted_iota(jnp.int32, (1, vocab_cols), 1)
    hit = columns == targets[:, None]
    target_local = jnp.sum(jnp.where(hit, logits, f32(0.0)), axis=1)
    top = jnp.max(logits, axis=1)
    total = jnp.sum(jnp.exp(logits - top[:, None]), axis=1)
    stats = lax.all_gather(jnp.stack([top, total, target_local]), ("expert", "mp"))
    tops, totals, hits = stats[:, 0], stats[:, 1], stats[:, 2]
    top_all = jnp.max(tops, axis=0)
    exp_total = jnp.sum(totals * jnp.exp(tops - top_all[None, :]), axis=0)
    log_probs = jnp.sum(hits, axis=0) - top_all - jnp.log(exp_total)
    return (mixed, log_probs)


HC = 256
LC = 512


def fused_kernel(
    tok_hbm, w_own, targets, wg_hbm, wu_hbm, wd_hbm, gain, lens_hbm,
    mixed_out, lp_out,
    tok, wts, wg, wu, wd, lens, h, acc, core_tx, core_rx, rs_tx, rs_rx, mix, xmix,
    gained, own_lg, lg_tx, lg_rx, stats,
    ld_sem, wg_sem, wu_sem, tok_s, tok_r, h_s, h_r, core_s, core_r,
    rs_s, rs_r, ag_s, ag_r, fw_s, fw_r, xm_s, xm_r, lg_s, lg_r, st_s, st_r,
):
    slab, feats = tok_hbm.shape
    hid = wg_hbm.shape[1]
    half = wd_hbm.shape[1]
    quarter = half // 2
    vocab = lens_hbm.shape[1]
    n_hc, n_lc = hid // HC, vocab // LC
    x, e, m = lax.axis_index("dp"), lax.axis_index("expert"), lax.axis_index("mp")
    n_mp = lax.axis_size("mp")
    n_plane = lax.axis_size("expert") * n_mp
    n_chip = n_plane // 2
    c = e % 2
    y = e // 2
    q = y * n_mp + m
    p = e * n_mp + m
    rb = 2 * slab // n_chip
    xp = 1 - x
    xdev = {"dp": xp}
    cdev = {"expert": y * 2 + 1 - c}

    def chip(d):
        t = (q + d) % n_chip
        return {"expert": (t // n_mp) * 2 + c, "mp": t % n_mp}

    def plane(d):
        t = (p + d) % n_plane
        return {"expert": t // n_mp, "mp": t % n_mp}

    def rcopy(src, dst, ss, rs, dev):
        return pltpu.make_async_remote_copy(
            src_ref=src, dst_ref=dst, send_sem=ss, recv_sem=rs,
            device_id=dev, device_id_type=pl.DeviceIdType.MESH,
        )

    def rows(who):
        return pl.ds(pl.multiple_of(who * slab, slab), slab)

    def lanes(start, size):
        return pl.ds(pl.multiple_of(start, 128), size)

    own_tok = pltpu.make_async_copy(tok_hbm, tok.at[rows(x)], ld_sem.at[0])
    own_tok.start()

    def wload(j):
        cols = lanes(j * HC, HC)
        return (
            pltpu.make_async_copy(wg_hbm.at[:, cols], wg.at[:, cols], wg_sem.at[j]),
            pltpu.make_async_copy(wu_hbm.at[:, cols], wu.at[:, cols], wu_sem.at[j]),
        )

    for j in range(n_hc):
        for copy in wload(j):
            copy.start()
    down_load = pltpu.make_async_copy(wd_hbm, wd, ld_sem.at[1])
    down_load.start()
    lens_load = pltpu.make_async_copy(lens_hbm, lens, ld_sem.at[2])
    lens_load.start()

    barrier = pltpu.get_barrier_semaphore()
    pl.semaphore_signal(barrier, inc=1, device_id=xdev, device_id_type=pl.DeviceIdType.MESH)
    for d in range(1, n_plane):
        pl.semaphore_signal(
            barrier, inc=1, device_id=plane(d), device_id_type=pl.DeviceIdType.MESH
        )
    own_tok.wait()
    pl.semaphore_wait(barrier, n_plane)

    sends = []
    part = slab // 2
    mine = tok.at[pl.ds(pl.multiple_of(x * slab + c * part, part), part)]
    tok_x = rcopy(mine, mine, tok_s.at[0], tok_r.at[0], xdev)
    tok_x.start()
    wts[rows(x), :] = w_own[...]
    w_x = rcopy(wts.at[rows(x)], wts.at[rows(x)], tok_s.at[2], tok_r.at[2], xdev)
    w_x.start()

    def hcopy(k, j):
        who = x if k == 0 else xp
        block = h.at[rows(who), lanes(x * hid + j * HC, HC)]
        return rcopy(block, block, h_s.at[k * n_hc + j], h_r.at[k * n_hc + j], xdev)

    def hidden_steps(k):
        who = x if k == 0 else xp

        def step(j, carry):
            if k == 0:
                for copy in wload(j):
                    copy.wait()
            t = tok[rows(who), :]
            cols = lanes(j * HC, HC)
            g = jnp.dot(t, wg[:, cols], preferred_element_type=f32)
            u = jnp.dot(t, wu[:, cols], preferred_element_type=f32)
            h[rows(who), lanes(x * hid + j * HC, HC)] = (jax.nn.silu(g) * u).astype(bf16)
            hcopy(k, j).start()
            return carry

        lax.fori_loop(0, n_hc, step, 0)

    tok_x.wait_recv()
    theirs = tok.at[pl.ds(pl.multiple_of(xp * slab + c * part, part), part)]
    tok_c = rcopy(theirs, theirs, tok_s.at[1], tok_r.at[1], cdev)
    tok_c.start()
    hidden_steps(0)
    tok_c.wait_recv()
    hidden_steps(1)

    down_load.wait()
    n_dc = half // HC

    def down_own(j, carry):
        cols = lanes(j * HC, HC)
        acc[:, cols] = jnp.dot(
            h[:, lanes(x * hid, hid)],
            wd[pl.ds(pl.multiple_of(x * hid, hid), hid), cols],
            preferred_element_type=f32,
        )
        return carry

    lax.fori_loop(0, n_dc, down_own, 0)
    w_x.wait_recv()

    def hwait(j, carry):
        hcopy(0, j).wait_recv()
        hcopy(1, j).wait_recv()
        return carry

    lax.fori_loop(0, n_hc, hwait, 0)

    def down_other(j, first):
        cols = lanes(first + j * HC, HC)
        more = jnp.dot(
            h[:, lanes(xp * hid, hid)],
            wd[pl.ds(pl.multiple_of(xp * hid, hid), hid), cols],
            preferred_element_type=f32,
        )
        return (acc[:, cols] + more) * wts[:, 0:1]

    def down_give(j, carry):
        core_tx[:, lanes(j * HC, HC)] = down_other(j, (1 - c) * quarter)
        return carry

    lax.fori_loop(0, n_dc // 2, down_give, 0)
    core_x = rcopy(core_tx, core_rx, core_s, core_r, cdev)
    core_x.start()

    def down_keep(j, carry):
        value = down_other(j, c * quarter)
        acc[:, lanes(c * quarter + j * HC, HC)] = value
        return carry

    lax.fori_loop(0, n_dc // 2, down_keep, 0)
    core_x.wait_recv()
    kept = lanes(c * quarter, quarter)
    core_rx[...] = core_rx[...] + acc[:, kept]
    rs_tx[...] = core_rx[...].astype(bf16)

    def blk(who):
        return pl.ds(pl.multiple_of(who * rb, rb), rb)

    rs = []
    for d in range(1, n_chip):
        copy = rcopy(
            rs_tx.at[blk((q + d) % n_chip)], rs_rx.at[d - 1], rs_s.at[d - 1], rs_r.at[d - 1], chip(d)
        )
        copy.start()
        rs.append(copy)
    total = core_rx[blk(q), :]
    total = total + tok[blk(q), lanes(x * half + c * quarter, quarter)].astype(f32)
    for d in range(1, n_chip):
        rs[d - 1].wait_recv()
        total = total + rs_rx[d - 1].astype(f32)
    mix[blk(q), kept] = total.astype(bf16)

    ag = []
    block = mix.at[blk(q), kept]
    for d in range(1, n_chip):
        copy = rcopy(block, block, ag_s.at[d - 1], ag_r.at[d - 1], chip(d))
        copy.start()
        ag.append(copy)
    fw = [rcopy(block, block, fw_s.at[0], fw_r.at[0], cdev)]
    fw[0].start()
    for d in range(1, n_chip):
        ag[d - 1].wait_recv()
        got = mix.at[blk((q + n_chip - d) % n_chip), kept]
        copy = rcopy(got, got, fw_s.at[d], fw_r.at[d], cdev)
        copy.start()
        fw.append(copy)
    xm = rcopy(mix.at[rows(xp), kept], xmix.at[:, kept], xm_s.at[0], xm_r.at[0], xdev)
    xm.start()
    for copy in fw:
        copy.wait_recv()
    gained[...] = (mix[...].astype(f32) * gain[:, lanes(x * half, half)]).astype(bf16)
    lens_load.wait()

    def lgcopy(j):
        cols = lanes(j * LC, LC)
        return rcopy(lg_tx.at[:, cols], lg_rx.at[:, cols], lg_s.at[j], lg_r.at[j], xdev)

    def logits_give(j, carry):
        cols = lanes(j * LC, LC)
        lg_tx[:, cols] = jnp.dot(
            gained[rows(xp), :], lens[:, cols], preferred_element_type=f32
        ).astype(bf16)
        lgcopy(j).start()
        return carry

    lax.fori_loop(0, n_lc, logits_give, 0)

    xm.wait_recv()
    xf = rcopy(xmix.at[:, kept], xmix.at[:, kept], xm_s.at[1], xm_r.at[1], cdev)
    xf.start()

    def logits_keep(j, carry):
        cols = lanes(j * LC, LC)
        own_lg[:, cols] = jnp.dot(
            gained[rows(x), :], lens[:, cols], preferred_element_type=f32
        )
        return carry

    lax.fori_loop(0, n_lc, logits_keep, 0)

    mine_mix = mix[rows(x), :]
    mixed_out[:, lanes(x * half, half)] = mine_mix
    xf.wait_recv()
    other_mix = xmix[...]
    mixed_out[:, lanes(xp * half, half)] = other_mix
    a, b = mine_mix.astype(f32), other_mix.astype(f32)
    square = jnp.sum(a * a, axis=1, keepdims=True) + jnp.sum(b * b, axis=1, keepdims=True)
    scale = lax.rsqrt(square / feats + 1e-05)

    top = jnp.full((slab, 1), -jnp.inf, f32)
    hit = jnp.zeros((slab, 1), f32)
    for j in range(n_lc):
        cols = pl.ds(j * LC, LC)
        lgcopy(j).wait_recv()
        value = (own_lg[:, cols] + lg_rx[:, cols].astype(f32)) * scale
        own_lg[:, cols] = value
        top = jnp.maximum(top, jnp.max(value, axis=1, keepdims=True))
        place = p * vocab + j * LC + lax.broadcasted_iota(jnp.int32, (slab, LC), 1)
        hit = hit + jnp.sum(
            jnp.where(place == targets[...], value, f32(0.0)), axis=1, keepdims=True
        )
    summed = jnp.zeros((slab, 1), f32)
    for j in range(n_lc):
        summed = summed + jnp.sum(
            jnp.exp(own_lg[:, pl.ds(j * LC, LC)] - top), axis=1, keepdims=True
        )
    lane = lax.broadcasted_iota(jnp.int32, (slab, 128), 1)
    packed = jnp.where(lane == 0, top, jnp.where(lane == 1, summed, hit))
    packed = jnp.concatenate([packed, packed], axis=0)
    stats[0] = packed.T[0:8, :]
    st = []
    for d in range(1, n_plane):
        copy = rcopy(stats.at[0], stats.at[d], st_s.at[d - 1], st_r.at[d - 1], plane(d))
        copy.start()
        st.append(copy)
    for copy in st:
        copy.wait_recv()
    every = stats[...]
    tops, sums, hits = every[:, 0:1, :], every[:, 1:2, :], every[:, 2:3, :]
    top_all = jnp.max(tops, axis=0)
    exp_total = jnp.sum(sums * jnp.exp(tops - top_all[None]), axis=0)
    result = jnp.sum(hits, axis=0) - top_all - jnp.log(exp_total)
    lp_out[...] = jnp.broadcast_to(result, lp_out.shape)

    for copy in [tok_x, w_x, tok_c, core_x, xm, xf] + rs + ag + fw + st:
        copy.wait_send()

    def hdone(j, carry):
        hcopy(0, j).wait_send()
        hcopy(1, j).wait_send()
        return carry

    lax.fori_loop(0, n_hc, hdone, 0)

    def lgdone(j, carry):
        lgcopy(j).wait_send()
        return carry

    lax.fori_loop(0, n_lc, lgdone, 0)


def per_device_fused(
    tokens, expert_ids, gate_values, targets, w_gate, w_up, w_down, norm_gain, lens_head
):
    slab, feats = tokens.shape
    owner = lax.axis_index("expert")
    weights = jnp.sum(jnp.where(expert_ids == owner, gate_values, f32(0.0)), axis=1)
    weights = jnp.broadcast_to(weights[:, None], (slab, 128))
    wg = w_gate.reshape(feats, -1)
    wu = w_up.reshape(feats, -1)
    wd = w_down.reshape(w_down.shape[2], w_down.shape[3])
    hid, half, vocab = wg.shape[1], wd.shape[1], lens_head.shape[1]
    n_plane = lax.axis_size("expert") * lax.axis_size("mp")
    n_chip = n_plane // 2
    all_rows = 2 * slab
    n_hc, n_lc = hid // HC, vocab // LC
    dma = pltpu.SemaphoreType.DMA
    vmem = pl.BlockSpec(memory_space=pltpu.VMEM)
    hbm = pl.BlockSpec(memory_space=pl.ANY)
    flops = 2 * all_rows * (2 * feats * hid + 2 * hid * half + half * vocab)
    mixed, lp = pl.pallas_call(
        fused_kernel,
        out_shape=(
            jax.ShapeDtypeStruct((slab, feats), bf16),
            jax.ShapeDtypeStruct((8, 128), f32),
        ),
        in_specs=[hbm, vmem, vmem, hbm, hbm, hbm, vmem, hbm],
        out_specs=(vmem, vmem),
        scratch_shapes=[
            pltpu.VMEM((all_rows, feats), bf16),
            pltpu.VMEM((all_rows, 128), f32),
            pltpu.VMEM(wg.shape, bf16),
            pltpu.VMEM(wu.shape, bf16),
            pltpu.VMEM(wd.shape, bf16),
            pltpu.VMEM(lens_head.shape, bf16),
            pltpu.VMEM((all_rows, 2 * hid), bf16),
            pltpu.VMEM((all_rows, half), f32),
            pltpu.VMEM((all_rows, half // 2), f32),
            pltpu.VMEM((all_rows, half // 2), f32),
            pltpu.VMEM((all_rows, half // 2), bf16),
            pltpu.VMEM((n_chip - 1, all_rows // n_chip, half // 2), bf16),
            pltpu.VMEM((all_rows, half), bf16),
            pltpu.VMEM((slab, half), bf16),
            pltpu.VMEM((all_rows, half), bf16),
            pltpu.VMEM((slab, vocab), f32),
            pltpu.VMEM((slab, vocab), bf16),
            pltpu.VMEM((slab, vocab), bf16),
            pltpu.VMEM((n_plane, 8, 128), f32),
            dma((3,)), dma((n_hc,)), dma((n_hc,)),
            dma((3,)), dma((3,)),
            dma((2 * n_hc,)), dma((2 * n_hc,)),
            dma, dma,
            dma((n_chip - 1,)), dma((n_chip - 1,)),
            dma((n_chip - 1,)), dma((n_chip - 1,)),
            dma((n_chip,)), dma((n_chip,)),
            dma((2,)), dma((2,)),
            dma((n_lc,)), dma((n_lc,)),
            dma((n_plane - 1,)), dma((n_plane - 1,)),
        ],
        compiler_params=pltpu.CompilerParams(
            collective_id=0, has_side_effects=True, vmem_limit_bytes=48 * 1024 * 1024
        ),
        cost_estimate=pl.CostEstimate(
            flops=flops, bytes_accessed=4 * wg.size * 2, transcendentals=0
        ),
    )(tokens, weights, targets[:, None], wg, wu, wd, norm_gain[None, :], lens_head)
    return (mixed, lp[0, :slab])


def solution(mesh):
    in_specs = (
        P("dp", None),
        P("dp", None),
        P("dp", None),
        P("dp"),
        P("expert", None, "mp", "dp"),
        P("expert", None, "mp", "dp"),
        P("expert", "mp", None, "dp"),
        P(),
        P("dp", ("expert", "mp")),
    )
    out_specs = (P("dp", None), P("dp"))
    fused = mesh.shape["dp"] == 2 and mesh.shape["expert"] == 4 and mesh.shape["mp"] == 4
    return jax.shard_map(
        per_device_fused if fused else per_device, mesh=mesh, in_specs=in_specs, out_specs=out_specs, check_vma=False
    )
```

```python
import jax
import jax.numpy as jnp
from jax import lax
from jax.experimental import pallas as pl
from jax.experimental.pallas import tpu as pltpu
from jax.sharding import PartitionSpec as P

f32, bf16 = jnp.float32, jnp.bfloat16


def per_device(
    tokens, expert_ids, gate_values, targets, w_gate, w_up, w_down, norm_gain, lens_head
):
    rows, feats = tokens.shape
    owner = lax.axis_index("expert")
    weights = jnp.sum(jnp.where(expert_ids == owner, gate_values, f32(0.0)), axis=1)
    gate_mat = w_gate.reshape(feats, -1)
    up_mat = w_up.reshape(feats, -1)
    down_mat = w_down.reshape(w_down.shape[2], w_down.shape[3])
    own_feats = down_mat.shape[1]
    all_tokens = lax.all_gather(tokens, "dp", axis=0, tiled=True)
    all_weights = lax.all_gather(weights, "dp", axis=0, tiled=True)
    gate_part = jnp.dot(all_tokens, gate_mat, preferred_element_type=f32)
    up_part = jnp.dot(all_tokens, up_mat, preferred_element_type=f32)
    hidden = (jax.nn.silu(gate_part) * up_part).astype(bf16)
    hidden = lax.all_gather(hidden, "dp", axis=1, tiled=True)
    part = jnp.dot(hidden, down_mat, preferred_element_type=f32) * all_weights[:, None]
    summed = lax.psum(part, ("expert", "mp"))
    first = lax.axis_index("dp") * own_feats
    own_tokens = lax.dynamic_slice_in_dim(all_tokens, first, own_feats, axis=1)
    own_gain = lax.dynamic_slice_in_dim(norm_gain, first, own_feats, axis=0)
    mixed_part = (own_tokens.astype(f32) + summed).astype(bf16)
    mixed = lax.all_to_all(mixed_part, "dp", split_axis=0, concat_axis=1, tiled=True)
    mixed_f = mixed.astype(f32)
    scale = lax.rsqrt(jnp.mean(mixed_f * mixed_f, axis=1) + 1e-05)
    gained = (mixed_part.astype(f32) * own_gain[None, :]).astype(bf16)
    logits_part = jnp.dot(gained, lens_head, preferred_element_type=f32)
    logits = lax.psum_scatter(logits_part, "dp", scatter_dimension=0, tiled=True)
    logits = logits * scale[:, None]
    vocab_cols = lens_head.shape[1]
    vocab_start = (owner * lax.axis_size("mp") + lax.axis_index("mp")) * vocab_cols
    columns = vocab_start + lax.broadcasted_iota(jnp.int32, (1, vocab_cols), 1)
    hit = columns == targets[:, None]
    target_local = jnp.sum(jnp.where(hit, logits, f32(0.0)), axis=1)
    top = jnp.max(logits, axis=1)
    total = jnp.sum(jnp.exp(logits - top[:, None]), axis=1)
    stats = lax.all_gather(jnp.stack([top, total, target_local]), ("expert", "mp"))
    tops, totals, hits = stats[:, 0], stats[:, 1], stats[:, 2]
    top_all = jnp.max(tops, axis=0)
    exp_total = jnp.sum(totals * jnp.exp(tops - top_all[None, :]), axis=0)
    log_probs = jnp.sum(hits, axis=0) - top_all - jnp.log(exp_total)
    return (mixed, log_probs)


HC = 256
LC = 512


def fused_kernel(
    tok_hbm, ids_hbm, gates_hbm, targets_hbm, wg_hbm, wu_hbm, wd_hbm, gain_hbm, lens_hbm,
    mixed_out, lp_out,
    tok, wts, wg, wu, wd, lens, h, acc, core_tx, core_rx, rs_tx, rs_rx, mix, xmix,
    gained, own_lg, lg_tx, lg_rx, stats, ids, gates, targets, gain,
    ld_sem, wg_sem, wu_sem, tok_s, tok_r, h_s, h_r, core_s, core_r,
    rs_s, rs_r, ag_s, ag_r, fw_s, fw_r, xm_s, xm_r, lg_s, lg_r, st_s, st_r,
):
    slab, feats = tok_hbm.shape
    hid = wg_hbm.shape[1]
    half = wd_hbm.shape[1]
    quarter = half // 2
    vocab = lens_hbm.shape[1]
    n_hc, n_lc = hid // HC, vocab // LC
    x, e, m = lax.axis_index("dp"), lax.axis_index("expert"), lax.axis_index("mp")
    n_mp = lax.axis_size("mp")
    n_plane = lax.axis_size("expert") * n_mp
    n_chip = n_plane // 2
    c = e % 2
    y = e // 2
    q = y * n_mp + m
    p = e * n_mp + m
    rb = 2 * slab // n_chip
    xp = 1 - x
    xdev = {"dp": xp}
    cdev = {"expert": y * 2 + 1 - c}

    def chip(d):
        t = (q + d) % n_chip
        return {"expert": (t // n_mp) * 2 + c, "mp": t % n_mp}

    def plane(d):
        t = (p + d) % n_plane
        return {"expert": t // n_mp, "mp": t % n_mp}

    def rcopy(src, dst, ss, rs, dev):
        return pltpu.make_async_remote_copy(
            src_ref=src, dst_ref=dst, send_sem=ss, recv_sem=rs,
            device_id=dev, device_id_type=pl.DeviceIdType.MESH,
        )

    def rows(who):
        return pl.ds(pl.multiple_of(who * slab, slab), slab)

    def lanes(start, size):
        return pl.ds(pl.multiple_of(start, 128), size)

    own_tok = pltpu.make_async_copy(tok_hbm, tok.at[rows(x)], ld_sem.at[0])
    own_tok.start()
    small = [
        pltpu.make_async_copy(ids_hbm, ids, ld_sem.at[3]),
        pltpu.make_async_copy(gates_hbm, gates, ld_sem.at[4]),
        pltpu.make_async_copy(targets_hbm, targets, ld_sem.at[5]),
        pltpu.make_async_copy(gain_hbm, gain, ld_sem.at[6]),
    ]
    for copy in small:
        copy.start()

    def wload(j):
        cols = lanes(j * HC, HC)
        return (
            pltpu.make_async_copy(wg_hbm.at[:, cols], wg.at[:, cols], wg_sem.at[j]),
            pltpu.make_async_copy(wu_hbm.at[:, cols], wu.at[:, cols], wu_sem.at[j]),
        )

    for j in range(n_hc):
        for copy in wload(j):
            copy.start()
    down_load = pltpu.make_async_copy(wd_hbm, wd, ld_sem.at[1])
    down_load.start()
    lens_load = pltpu.make_async_copy(lens_hbm, lens, ld_sem.at[2])
    lens_load.start()

    barrier = pltpu.get_barrier_semaphore()
    pl.semaphore_signal(barrier, inc=1, device_id=xdev, device_id_type=pl.DeviceIdType.MESH)
    for d in range(1, n_plane):
        pl.semaphore_signal(
            barrier, inc=1, device_id=plane(d), device_id_type=pl.DeviceIdType.MESH
        )
    own_tok.wait()
    pl.semaphore_wait(barrier, n_plane)

    sends = []
    part = slab // 2
    mine = tok.at[pl.ds(pl.multiple_of(x * slab + c * part, part), part)]
    tok_x = rcopy(mine, mine, tok_s.at[0], tok_r.at[0], xdev)
    tok_x.start()
    for copy in small:
        copy.wait()
    w_row = jnp.sum(jnp.where(ids[...] == e, gates[...], f32(0.0)), axis=0, keepdims=True)
    eye = lax.broadcasted_iota(jnp.int32, (slab, slab), 0) == lax.broadcasted_iota(
        jnp.int32, (slab, slab), 1
    )

    def column(row, zero):
        return jnp.sum(
            jnp.where(eye, jnp.broadcast_to(row, (slab, slab)), zero), axis=1, keepdims=True
        )

    wts[rows(x), :] = jnp.broadcast_to(column(w_row, f32(0.0)), (slab, 128))
    w_x = rcopy(wts.at[rows(x)], wts.at[rows(x)], tok_s.at[2], tok_r.at[2], xdev)
    w_x.start()

    def hcopy(k, j):
        who = x if k == 0 else xp
        block = h.at[rows(who), lanes(x * hid + j * HC, HC)]
        return rcopy(block, block, h_s.at[k * n_hc + j], h_r.at[k * n_hc + j], xdev)

    def hidden_steps(k, first, last):
        who = x if k == 0 else xp

        def step(j, carry):
            if k == 0:
                for copy in wload(j):
                    copy.wait()
            t = tok[rows(who), :]
            cols = lanes(j * HC, HC)
            g = jnp.dot(t, wg[:, cols], preferred_element_type=f32)
            u = jnp.dot(t, wu[:, cols], preferred_element_type=f32)
            h[rows(who), lanes(x * hid + j * HC, HC)] = (jax.nn.silu(g) * u).astype(bf16)
            hcopy(k, j).start()
            return carry

        lax.fori_loop(first, last, step, 0)

    hidden_steps(0, 0, n_hc // 2)
    tok_x.wait_recv()
    theirs = tok.at[pl.ds(pl.multiple_of(xp * slab + c * part, part), part)]
    tok_c = rcopy(theirs, theirs, tok_s.at[1], tok_r.at[1], cdev)
    tok_c.start()
    hidden_steps(0, n_hc // 2, n_hc)
    tok_c.wait_recv()
    hidden_steps(1, 0, n_hc)

    down_load.wait()
    n_dc = half // HC

    def down_own(j, carry):
        cols = lanes(j * HC, HC)
        acc[:, cols] = jnp.dot(
            h[:, lanes(x * hid, hid)],
            wd[pl.ds(pl.multiple_of(x * hid, hid), hid), cols],
            preferred_element_type=f32,
        )
        return carry

    lax.fori_loop(0, n_dc, down_own, 0)
    w_x.wait_recv()

    def hwait(j, carry):
        hcopy(0, j).wait_recv()
        hcopy(1, j).wait_recv()
        return carry

    lax.fori_loop(0, n_hc, hwait, 0)

    def down_other(j, first):
        cols = lanes(first + j * HC, HC)
        more = jnp.dot(
            h[:, lanes(xp * hid, hid)],
            wd[pl.ds(pl.multiple_of(xp * hid, hid), hid), cols],
            preferred_element_type=f32,
        )
        return (acc[:, cols] + more) * wts[:, 0:1]

    def core_x(j):
        cols = lanes(j * HC, HC)
        return rcopy(core_tx.at[:, cols], core_rx.at[:, cols], core_s.at[j], core_r.at[j], cdev)

    def down_give(j, carry):
        core_tx[:, lanes(j * HC, HC)] = down_other(j, (1 - c) * quarter)
        core_x(j).start()
        return carry

    lax.fori_loop(0, n_dc // 2, down_give, 0)

    def blk(who):
        return pl.ds(pl.multiple_of(who * rb, rb), rb)

    kept = lanes(c * quarter, quarter)
    n_q = n_dc // 2

    def rs_copy(j, d):
        cols = lanes(j * HC, HC)
        spot = (d - 1) * n_q + j
        return rcopy(
            rs_tx.at[blk((q + d) % n_chip), cols], rs_rx.at[d - 1, :, cols],
            rs_s.at[spot], rs_r.at[spot], chip(d),
        )

    def down_keep(j, carry):
        cols = lanes(j * HC, HC)
        value = down_other(j, c * quarter)
        core_x(j).wait_recv()
        value = value + core_rx[:, cols]
        core_rx[:, cols] = value
        rs_tx[:, cols] = value.astype(bf16)
        for d in range(1, n_chip):
            rs_copy(j, d).start()
        return carry

    lax.fori_loop(0, n_q, down_keep, 0)
    total = core_rx[blk(q), :]
    total = total + tok[blk(q), lanes(x * half + c * quarter, quarter)].astype(f32)
    for d in range(1, n_chip):
        for j in range(n_q):
            rs_copy(j, d).wait_recv()
        total = total + rs_rx[d - 1].astype(f32)
    mix[blk(q), kept] = total.astype(bf16)

    ag = []
    block = mix.at[blk(q), kept]
    for d in range(1, n_chip):
        copy = rcopy(block, block, ag_s.at[d - 1], ag_r.at[d - 1], chip(d))
        copy.start()
        ag.append(copy)
    fw = [rcopy(block, block, fw_s.at[0], fw_r.at[0], cdev)]
    fw[0].start()
    for d in range(1, n_chip):
        ag[d - 1].wait_recv()
        got = mix.at[blk((q + n_chip - d) % n_chip), kept]
        copy = rcopy(got, got, fw_s.at[d], fw_r.at[d], cdev)
        copy.start()
        fw.append(copy)
    xm = rcopy(mix.at[rows(xp), kept], xmix.at[:, kept], xm_s.at[0], xm_r.at[0], xdev)
    xm.start()
    for copy in fw:
        copy.wait_recv()
    gained[...] = (mix[...].astype(f32) * gain[:, lanes(x * half, half)]).astype(bf16)
    lens_load.wait()

    def lgcopy(j):
        cols = lanes(j * LC, LC)
        return rcopy(lg_tx.at[:, cols], lg_rx.at[:, cols], lg_s.at[j], lg_r.at[j], xdev)

    def logits_give(j, carry):
        cols = lanes(j * LC, LC)
        lg_tx[:, cols] = jnp.dot(
            gained[rows(xp), :], lens[:, cols], preferred_element_type=f32
        ).astype(bf16)
        lgcopy(j).start()
        return carry

    lax.fori_loop(0, n_lc, logits_give, 0)

    xm.wait_recv()
    xf = rcopy(xmix.at[:, kept], xmix.at[:, kept], xm_s.at[1], xm_r.at[1], cdev)
    xf.start()

    def logits_keep(j, carry):
        cols = lanes(j * LC, LC)
        own_lg[:, cols] = jnp.dot(
            gained[rows(x), :], lens[:, cols], preferred_element_type=f32
        )
        return carry

    lax.fori_loop(0, n_lc, logits_keep, 0)

    mine_mix = mix[rows(x), :]
    mixed_out[:, lanes(x * half, half)] = mine_mix
    xf.wait_recv()
    other_mix = xmix[...]
    mixed_out[:, lanes(xp * half, half)] = other_mix
    a, b = mine_mix.astype(f32), other_mix.astype(f32)
    square = jnp.sum(a * a, axis=1, keepdims=True) + jnp.sum(b * b, axis=1, keepdims=True)
    scale = lax.rsqrt(square / feats + 1e-05)

    wanted = column(targets[...], 0) - p * vocab
    top = jnp.full((slab, 1), -jnp.inf, f32)
    hit = jnp.zeros((slab, 1), f32)
    for j in range(n_lc):
        cols = pl.ds(j * LC, LC)
        lgcopy(j).wait_recv()
        value = (own_lg[:, cols] + lg_rx[:, cols].astype(f32)) * scale
        own_lg[:, cols] = value
        top = jnp.maximum(top, jnp.max(value, axis=1, keepdims=True))
        place = j * LC + lax.broadcasted_iota(jnp.int32, (slab, LC), 1)
        hit = hit + jnp.sum(
            jnp.where(place == wanted, value, f32(0.0)), axis=1, keepdims=True
        )
    summed = jnp.zeros((slab, 1), f32)
    for j in range(n_lc):
        summed = summed + jnp.sum(
            jnp.exp(own_lg[:, pl.ds(j * LC, LC)] - top), axis=1, keepdims=True
        )
    lane = lax.broadcasted_iota(jnp.int32, (slab, 128), 1)
    packed = jnp.where(lane == 0, top, jnp.where(lane == 1, summed, hit))
    packed = jnp.concatenate([packed, packed], axis=0)
    stats[0] = packed.T[0:8, :]
    st = []
    for d in range(1, n_plane):
        copy = rcopy(stats.at[0], stats.at[d], st_s.at[d - 1], st_r.at[d - 1], plane(d))
        copy.start()
        st.append(copy)
    for copy in st:
        copy.wait_recv()
    every = stats[...]
    tops, sums, hits = every[:, 0:1, :], every[:, 1:2, :], every[:, 2:3, :]
    top_all = jnp.max(tops, axis=0)
    exp_total = jnp.sum(sums * jnp.exp(tops - top_all[None]), axis=0)
    result = jnp.sum(hits, axis=0) - top_all - jnp.log(exp_total)
    lp_out[...] = jnp.broadcast_to(result, lp_out.shape)

    for j in range(n_q):
        core_x(j).wait_send()
        for d in range(1, n_chip):
            rs_copy(j, d).wait_send()
    for copy in [tok_x, w_x, tok_c, xm, xf] + ag + fw + st:
        copy.wait_send()

    def hdone(j, carry):
        hcopy(0, j).wait_send()
        hcopy(1, j).wait_send()
        return carry

    lax.fori_loop(0, n_hc, hdone, 0)

    def lgdone(j, carry):
        lgcopy(j).wait_send()
        return carry

    lax.fori_loop(0, n_lc, lgdone, 0)


def per_device_fused(
    tokens, expert_ids, gate_values, targets, w_gate, w_up, w_down, norm_gain, lens_head
):
    slab, feats = tokens.shape
    wg = w_gate.reshape(feats, -1)
    wu = w_up.reshape(feats, -1)
    wd = w_down.reshape(w_down.shape[2], w_down.shape[3])
    hid, half, vocab = wg.shape[1], wd.shape[1], lens_head.shape[1]
    n_plane = lax.axis_size("expert") * lax.axis_size("mp")
    n_chip = n_plane // 2
    all_rows = 2 * slab
    n_hc, n_lc = hid // HC, vocab // LC
    dma = pltpu.SemaphoreType.DMA
    vmem = pl.BlockSpec(memory_space=pltpu.VMEM)
    hbm = pl.BlockSpec(memory_space=pltpu.HBM)
    flops = 2 * all_rows * (2 * feats * hid + 2 * hid * half + half * vocab)
    mixed, lp = pl.pallas_call(
        fused_kernel,
        out_shape=(
            jax.ShapeDtypeStruct((slab, feats), bf16),
            jax.ShapeDtypeStruct((8, 128), f32),
        ),
        in_specs=[hbm] * 9,
        out_specs=(vmem, vmem),
        scratch_shapes=[
            pltpu.VMEM((all_rows, feats), bf16),
            pltpu.VMEM((all_rows, 128), f32),
            pltpu.VMEM(wg.shape, bf16),
            pltpu.VMEM(wu.shape, bf16),
            pltpu.VMEM(wd.shape, bf16),
            pltpu.VMEM(lens_head.shape, bf16),
            pltpu.VMEM((all_rows, 2 * hid), bf16),
            pltpu.VMEM((all_rows, half), f32),
            pltpu.VMEM((all_rows, half // 2), f32),
            pltpu.VMEM((all_rows, half // 2), f32),
            pltpu.VMEM((all_rows, half // 2), bf16),
            pltpu.VMEM((n_chip - 1, all_rows // n_chip, half // 2), bf16),
            pltpu.VMEM((all_rows, half), bf16),
            pltpu.VMEM((slab, half), bf16),
            pltpu.VMEM((all_rows, half), bf16),
            pltpu.VMEM((slab, vocab), f32),
            pltpu.VMEM((slab, vocab), bf16),
            pltpu.VMEM((slab, vocab), bf16),
            pltpu.VMEM((n_plane, 8, 128), f32),
            pltpu.VMEM((2, slab), jnp.int32),
            pltpu.VMEM((2, slab), f32),
            pltpu.VMEM((1, slab), jnp.int32),
            pltpu.VMEM((1, feats), f32),
            dma((7,)), dma((n_hc,)), dma((n_hc,)),
            dma((3,)), dma((3,)),
            dma((2 * n_hc,)), dma((2 * n_hc,)),
            dma((half // HC // 2,)), dma((half // HC // 2,)),
            dma(((n_chip - 1) * (half // HC // 2),)), dma(((n_chip - 1) * (half // HC // 2),)),
            dma((n_chip - 1,)), dma((n_chip - 1,)),
            dma((n_chip,)), dma((n_chip,)),
            dma((2,)), dma((2,)),
            dma((n_lc,)), dma((n_lc,)),
            dma((n_plane - 1,)), dma((n_plane - 1,)),
        ],
        compiler_params=pltpu.CompilerParams(
            collective_id=0, has_side_effects=True, vmem_limit_bytes=63_060_000
        ),
        cost_estimate=pl.CostEstimate(
            flops=flops, bytes_accessed=4 * wg.size * 2, transcendentals=0
        ),
    )(
        tokens, expert_ids.T, gate_values.T, targets[None, :], wg, wu, wd,
        norm_gain[None, :], lens_head,
    )
    return (mixed, lp[0, :slab])


def solution(mesh):
    in_specs = (
        P("dp", None),
        P("dp", None),
        P("dp", None),
        P("dp"),
        P("expert", None, "mp", "dp"),
        P("expert", None, "mp", "dp"),
        P("expert", "mp", None, "dp"),
        P(),
        P("dp", ("expert", "mp")),
    )
    out_specs = (P("dp", None), P("dp"))
    fused = mesh.shape["dp"] == 2 and mesh.shape["expert"] == 4 and mesh.shape["mp"] == 4
    return jax.shard_map(
        per_device_fused if fused else per_device, mesh=mesh, in_specs=in_specs, out_specs=out_specs, check_vma=False
    )
```
